32 devices in a mesh: row: 4 (over y, core), col: 8 (over z, x).
Axes of the slice: x: 2, y: 2, z: 4, core: 2. Of those that a mesh axis runs over, the one named last changes fastest.
Arguments:
- latent: bfloat16 [4, 16, 32, 320], P(None, 'row', 'col'), may hold values from -6 to 6
- conv_weight: bfloat16 [2, 3, 3, 320, 320], replicated, may hold values from -0.109375 to 0.109375
- conv_gain: float32 [2, 320], replicated, may hold values from 0.25 to 1.75
- qkv_weight: bfloat16 [3, 512, 320], P(None, 'col'), may hold values from -0.3125 to 0.3125
- qk_gain: bfloat16 [2, 512], P(None, 'col'), may hold values from 0.6 to 9, as said below
- out_weight: bfloat16 [512, 320], P('col'), may hold values from -0.5 to 0.5
Outputs:
- features: bfloat16 [4, 16, 32, 320], P(None, 'row', 'col')
- mixed: bfloat16 [4, 8, 16, 320], P('row', None, 'col')
The draws below stay inside these ranges and needn't reach their ends.
Inputs may be any that keep to these rules, and one draw needn't show every extreme that they name: `qk_gain`: positive gains.
All inputs are finite; a program needn't handle non-finite values.
Results may differ from the reference program's by a relative error of at most 0.035.
Values may be sent and summed in bfloat16 or wider, within the bound.
A program may use at most 64 MiB of HBM per device.

```python
import math
import jax
import jax.numpy as jnp
from jax import lax

C = 320
HD = 128
LAYERS = 2
IMAGES = 4
HEADS = 4
DM = 512
H0 = 16
W0 = 32
H1 = 8
W1 = 16
KEYS = 128


def draw_qk_gain(key, part):
    key_base = jax.random.fold_in(key, 0)
    base_gain = jnp.exp(jax.random.uniform(key_base, (2, DM), jnp.float32, math.log(0.6), math.log(1.8)))
    return base_gain.astype(jnp.bfloat16)


def block_levels(own_key, extent, cuts, low, largest):
    factor_of, own = 1.0, jax.random.fold_in(own_key, 6)
    for axis_at, parts in cuts:
        steps = jnp.exp(jax.random.uniform(jax.random.fold_in(own, axis_at), (parts,), jnp.float32, low / len(cuts), largest / len(cuts)))
        factor_of = factor_of * jnp.repeat(steps, extent[axis_at] // parts).reshape([-1 if axis == axis_at else 1 for axis in range(len(extent))])
    return factor_of


def gaussian(key, dims, deviation, bound, shards=(), held_as=jnp.bfloat16):
    factor_of = block_levels(key, dims, shards, -0.22, 0.18) if shards else 1.0
    entries = jax.random.normal(key, dims, jnp.float32) * deviation * factor_of
    return jnp.minimum(jnp.maximum(entries, -bound), bound).astype(held_as)


def setup_inputs(seed: int = 0) -> dict:
    keys = jax.random.split(jax.random.key(seed), 7)
    latent = gaussian(keys[0], (IMAGES, H0, W0, C), 1.0, 6.0, ((1, 4), (2, 8)))
    conv_weight = gaussian(keys[1], (LAYERS, 3, 3, C, C), (9 * C) ** -0.5, 0.109375)
    conv_gain = jnp.clip(1.0 + 0.15 * jax.random.normal(keys[2], (LAYERS, C), jnp.float32), 0.25, 1.75)
    qkv_weight = gaussian(keys[3], (3, DM, C), C ** -0.5, 0.3125, ((1, 8),))
    qk_gain = draw_qk_gain(jax.random.fold_in(keys[6], 71), 0)
    out_weight = gaussian(keys[5], (DM, C), HD ** -0.5, 0.5, ((0, 8),))
    return dict(latent=latent, conv_weight=conv_weight, conv_gain=conv_gain, qkv_weight=qkv_weight, qk_gain=qk_gain, out_weight=out_weight)


def rms_silu(hidden, gain_row):
    factor = lax.rsqrt(lax.optimization_barrier(jnp.mean(hidden * hidden, axis=-1, keepdims=True)) + 1e-06)
    return jax.nn.silu(hidden * factor * gain_row.astype(jnp.float32)).astype(jnp.bfloat16)

def conv_wrap(activation, kernels):
    height, width, channels = activation.shape
    total = jnp.zeros((height * width, kernels.shape[-1]), jnp.float32)
    for row_tap in range(3):
        for col_tap in range(3):
            moved = jnp.roll(activation, (1 - row_tap, 1 - col_tap), axis=(0, 1))
            total = total + jnp.dot(moved.reshape(height * width, channels), kernels[row_tap, col_tap], preferred_element_type=jnp.float32)
    return total.reshape(height, width, kernels.shape[-1])

def head_norm(projected, gain_row):
    factor = lax.rsqrt(lax.optimization_barrier(jnp.mean(projected * projected, axis=-1, keepdims=True)) + 1e-06)
    return (projected * factor * gain_row.astype(jnp.float32)).astype(jnp.bfloat16)

def project(source, matrix):
    return lax.dot_general(source, matrix, (((1,), (1,)), ((), ())), preferred_element_type=jnp.float32)

def reference(latent, conv_weight, conv_gain, qkv_weight, qk_gain, out_weight):
    head_weights = qkv_weight.reshape(3, HEADS, HD, C).transpose(1, 0, 2, 3)
    head_gains = qk_gain.reshape(2, HEADS, HD).transpose(1, 0, 2)
    head_out = out_weight.reshape(HEADS, HD, C)
    block_rows = math.gcd(KEYS, 512)
    scale = HD ** (-0.5)

    def one_image(image):
        hidden = image
        for layer_index in range(LAYERS):
            activation = rms_silu(hidden.astype(jnp.float32), conv_gain[layer_index])
            hidden = (hidden.astype(jnp.float32) + conv_wrap(activation, conv_weight[layer_index])).astype(jnp.bfloat16)
        pooled = hidden.astype(jnp.float32).reshape(H1, 2, W1, 2, C).mean(axis=(1, 3)).astype(jnp.bfloat16)
        token_rows = pooled.reshape(KEYS, C)

        def one_head(total, inputs):
            matrices, gains, out_rows = inputs
            query_norm = head_norm(project(token_rows, matrices[0]), gains[0])
            key_norm = head_norm(project(token_rows, matrices[1]), gains[1])
            value_rows = project(token_rows, matrices[2]).astype(jnp.bfloat16)

            def one_block(query_block):
                scores = jnp.dot(query_block, key_norm.T, preferred_element_type=jnp.float32) * scale
                shifted = jnp.exp(scores - lax.optimization_barrier(jnp.max(scores, axis=1, keepdims=True)))
                attended = jnp.dot(shifted.astype(jnp.bfloat16), value_rows, preferred_element_type=jnp.float32) / lax.optimization_barrier(jnp.sum(shifted, axis=1, keepdims=True))
                return jnp.dot(attended.astype(jnp.bfloat16), out_rows, preferred_element_type=jnp.float32)
            outputs = lax.map(one_block, query_norm.reshape(KEYS // block_rows, block_rows, HD))
            return (total + outputs.reshape(KEYS, C), None)
        summed, _ = lax.scan(one_head, jnp.zeros((KEYS, C), jnp.float32), (head_weights, head_gains, head_out))
        mixed = (token_rows.astype(jnp.float32) + summed).astype(jnp.bfloat16).reshape(H1, W1, C)
        return (hidden, mixed)
    features, mixed = lax.map(one_image, latent)
    return (features, mixed)
```

```python
import functools

import jax
import jax.numpy as jnp
import numpy as np
from jax import lax
from jax.experimental import pallas as pl
from jax.experimental.pallas import tpu as pltpu
from jax.sharding import PartitionSpec as P

MESH = pl.DeviceIdType.MESH
SIDES = [(0, 1), (0, -1), (1, 0), (-1, 0), (1, 1), (1, -1), (-1, 1), (-1, -1)]


def edge_source(step, tile, width):
    return {-1: range(width), 1: range(tile - width, tile), 0: range(tile)}[step]


def edge_target(step, tile, width):
    return {
        -1: range(width + tile, tile + 2 * width),
        1: range(width),
        0: range(width, width + tile),
    }[step]


def plan(images, tile_rows, tile_cols, width):
    ext_rows, ext_cols = tile_rows + 2 * width, tile_cols + 2 * width
    own_count = images * tile_rows * tile_cols

    def own_at(n, i, j):
        return (n * tile_rows + i) * tile_cols + j

    def ext_at(n, i, j):
        return (i * images + n) * ext_cols + j

    pack, segments, placed = [], [], np.zeros(images * ext_rows * ext_cols, np.int64)
    for n in range(images):
        for i in range(tile_rows):
            for j in range(tile_cols):
                placed[ext_at(n, i + width, j + width)] = own_at(n, i, j)
    for dr, dc in SIDES:
        start = len(pack)
        pairs = zip(edge_source(dr, tile_rows, width), edge_target(dr, tile_rows, width))
        for i, ti in pairs:
            for n in range(images):
                cols = zip(edge_source(dc, tile_cols, width), edge_target(dc, tile_cols, width))
                for j, tj in cols:
                    placed[ext_at(n, ti, tj)] = own_count + len(pack)
                    pack.append(own_at(n, i, j))
        segments.append((start, len(pack) - start))
    pack_matrix = np.eye(own_count)[np.array(pack)]
    place_matrix = np.eye(own_count + len(pack))[placed]
    read = np.zeros((own_count + own_count // 4, images * tile_rows * ext_cols))
    for n in range(images):
        for i in range(tile_rows):
            for j in range(tile_cols):
                at = ext_at(n, i, j + width)
                read[own_at(n, i, j), at] = 1.0
                token = (n * (tile_rows // 2) + i // 2) * (tile_cols // 2) + j // 2
                read[own_count + token, at] = 0.25
    return pack_matrix, place_matrix, read, segments


def dot(a, b):
    return jnp.dot(a, b, preferred_element_type=jnp.float32)


def dot_t(a, b):
    return lax.dot_general(a, b, (((1,), (1,)), ((), ())), preferred_element_type=jnp.float32)


def kernel(
    sizes,
    segments,
    own_ref, conv_hbm, gain_ref, qkv_hbm, qk_gain_ref, out_hbm, pack_ref, place_ref, read_ref,
    features_ref, mixed_ref,
    conv_w, shifted_act, border, around, qkv_w, out_w, head_gain, pooled_own, pooled_all,
    tokens, terms, returned,
    conv_sem, local_sem, halo_send, halo_recv, weight_send, weight_recv,
    pool_send, pool_recv, back_send, back_recv,
):
    images, tile_rows, tile_cols, layers, row_count, col_count = sizes
    ext_rows, ext_cols = tile_rows + 2 * layers, tile_cols + 2 * layers
    channels = own_ref.shape[1]
    own_count = own_ref.shape[0]
    devices = row_count * col_count
    me_r, me_c = lax.axis_index("row"), lax.axis_index("col")
    me = me_r * col_count + me_c
    half = lax.rem(me_c, 2)
    head = me_c // 2
    partner = (me_r, me_c + 1 - 2 * half)

    def other(step):
        to = lax.rem(me + step, devices)
        return to // col_count, lax.rem(to, col_count)

    barrier = pltpu.get_barrier_semaphore()

    def greet(step, _):
        pl.semaphore_signal(barrier, inc=1, device_id=other(step), device_id_type=MESH)
        return 0

    lax.fori_loop(1, devices, greet, 0)
    own_qkv = pltpu.make_async_copy(qkv_hbm, qkv_w.at[half], local_sem.at[0])
    own_out = pltpu.make_async_copy(out_hbm, out_w.at[half], local_sem.at[1])
    own_qkv.start()
    own_out.start()
    conv_copies = []
    for layer in range(layers):
        for a in range(3):
            at = layer * 3 + a
            copy = pltpu.make_async_copy(conv_hbm.at[layer, a], conv_w.at[layer, a], conv_sem.at[at])
            copy.start()
            conv_copies.append(copy)

    border[...] = dot(pack_ref[...], own_ref[...]).astype(jnp.bfloat16)
    around[:own_count] = own_ref[...]
    head_gain[half] = jnp.zeros(head_gain.shape[1:], jnp.float32)
    head_gain[half, :2, : qk_gain_ref.shape[1]] = qk_gain_ref[...].astype(jnp.float32)
    pl.semaphore_wait(barrier, devices - 1)

    halo_copies = []
    for k, (dr, dc) in enumerate(SIDES):
        start, count = segments[k]
        to = (lax.rem(me_r + dr + row_count, row_count), lax.rem(me_c + dc + col_count, col_count))
        copy = pltpu.make_async_remote_copy(
            src_ref=border.at[pl.ds(start, count)],
            dst_ref=around.at[pl.ds(own_count + start, count)],
            send_sem=halo_send.at[k],
            recv_sem=halo_recv.at[k],
            device_id=to,
            device_id_type=MESH,
        )
        copy.start()
        halo_copies.append(copy)
    own_qkv.wait()
    own_out.wait()
    weight_copies = []
    for k, ref in enumerate((qkv_w, out_w, head_gain)):
        copy = pltpu.make_async_remote_copy(
            src_ref=ref.at[half],
            dst_ref=ref.at[half],
            send_sem=weight_send.at[k],
            recv_sem=weight_recv.at[k],
            device_id=partner,
            device_id_type=MESH,
        )
        copy.start()
        weight_copies.append(copy)
    for copy in halo_copies:
        copy.wait_recv()

    hidden = dot(place_ref[...], around[...])
    line = images * ext_cols
    for layer in range(layers):
        factor = lax.rsqrt(jnp.mean(hidden * hidden, axis=-1, keepdims=True) + 1e-06)
        act = jax.nn.silu(hidden * factor * gain_ref[layer : layer + 1, :])
        rows = act.shape[0]
        groups = act.reshape(rows // ext_cols, ext_cols, channels)
        for b in range(3):
            moved = groups if b == 1 else pltpu.roll(groups, (1 - b) % ext_cols, axis=1)
            shifted_act[b, :rows] = moved.reshape(rows, channels).astype(jnp.bfloat16)
        inner = rows - 2 * line
        total = jnp.zeros((inner, channels), jnp.float32)
        for a in range(3):
            conv_copies[layer * 3 + a].wait()
            for b in range(3):
                total = total + dot(shifted_act[b, a * line : a * line + inner], conv_w[layer, a, b])
        rounded = (hidden[line : line + inner] + total).astype(jnp.bfloat16)
        hidden = rounded.astype(jnp.float32)

    both = dot(read_ref[...], rounded)
    features_ref[...] = both[:own_count].astype(jnp.bfloat16)
    pooled = both[own_count:].astype(jnp.bfloat16).astype(jnp.float32)
    tile_tokens = pooled_own.shape[1]
    for n in range(images):
        pooled_own[n] = pooled[n * tile_tokens : (n + 1) * tile_tokens]

    slot = me_c * row_count + me_r

    def scatter(step, _):
        to = other(step)
        pltpu.make_async_remote_copy(
            src_ref=pooled_own.at[to[0]],
            dst_ref=pooled_all.at[slot],
            send_sem=pool_send,
            recv_sem=pool_recv,
            device_id=to,
            device_id_type=MESH,
        ).start()
        return 0

    lax.fori_loop(1, devices, scatter, 0)
    pooled_all[slot] = pooled_own[me_r]
    for copy in weight_copies:
        copy.wait_recv()
    arrived = pltpu.make_async_remote_copy(
        src_ref=pooled_all.at[pl.ds(0, devices - 1)],
        dst_ref=pooled_all.at[pl.ds(0, devices - 1)],
        send_sem=pool_send,
        recv_sem=pool_recv,
        device_id=partner,
        device_id_type=MESH,
    )
    arrived.wait_recv()

    def join(i):
        return jnp.concatenate([pooled_all[2 * i], pooled_all[2 * i + 1]], axis=0)

    if devices <= 64:
        for i in range(devices // 2):
            tokens[8 * i : 8 * i + 8] = join(i)
    else:

        def put(i, _):
            tokens[pl.ds(pl.multiple_of(8 * i, 8), 8)] = join(i)
            return 0

        lax.fori_loop(0, devices // 2, put, 0)

    head_dim = 2 * qkv_w.shape[2]

    def head_matrix(part):
        return qkv_w[:, part].reshape(head_dim, channels)

    gains = head_gain[0] + pltpu.roll(head_gain[1], head_dim // 2, axis=1)

    def head_norm(projected, gain_row):
        factor = lax.rsqrt(jnp.mean(projected * projected, axis=-1, keepdims=True) + 1e-06)
        return (projected * factor * gain_row).astype(jnp.bfloat16)

    count = tokens.shape[0]
    queries = count // 2
    image_tokens = tokens[...].astype(jnp.bfloat16)
    key_norm = head_norm(dot_t(image_tokens, head_matrix(1)), gains[1:2])
    value_rows = dot_t(image_tokens, head_matrix(2)).astype(jnp.bfloat16)
    block = min(queries, 128)
    strip = terms.shape[1]

    def attend(at):
        first = half * queries + at * block
        rows = tokens[pl.ds(pl.multiple_of(first, block), block)].astype(jnp.bfloat16)
        query_norm = head_norm(dot_t(rows, head_matrix(0)), gains[0:1])
        scores = dot_t(query_norm, key_norm) * head_dim ** (-0.5)
        shifted = jnp.exp(scores - jnp.max(scores, axis=1, keepdims=True))
        out = dot(shifted.astype(jnp.bfloat16), value_rows)
        return (out / jnp.sum(shifted, axis=1, keepdims=True)).astype(jnp.bfloat16)

    out_rows = out_w[...].reshape(head_dim, channels)

    def one_block(at):
        term = dot(attend(at), out_rows).astype(jnp.bfloat16)
        for k in range(block // strip):
            terms[at * (block // strip) + k] = term[k * strip : (k + 1) * strip]

    if queries == block:
        one_block(0)
    else:

        def step(at, _):
            one_block(at)
            return 0

        lax.fori_loop(0, queries // block, step, 0)

    heads = col_count // 2

    def back(k):
        return pltpu.make_async_remote_copy(
            src_ref=terms.at[k],
            dst_ref=returned.at[head],
            send_sem=back_send.at[k],
            recv_sem=back_recv.at[head],
            device_id=(me_r, half * heads + k),
            device_id_type=MESH,
        )

    for k in range(heads):

        @pl.when(half * heads + k != me_c)
        def _():
            back(k).start()

        @pl.when(half * heads + k == me_c)
        def _():
            returned[head] = terms[k]

    mine = tokens[pl.ds(pl.multiple_of(me_c * strip, strip), strip)]
    for h in range(heads):

        @pl.when(2 * h + me_c // heads != me_c)
        def _():
            pltpu.make_async_remote_copy(
                src_ref=terms.at[0],
                dst_ref=returned.at[h],
                send_sem=back_send.at[0],
                recv_sem=back_recv.at[h],
                device_id=partner,
                device_id_type=MESH,
            ).wait_recv()

    total = returned[0].astype(jnp.float32)
    for h in range(1, heads):
        total = total + returned[h].astype(jnp.float32)
    mixed_ref[...] = (mine + total).astype(jnp.bfloat16)

    for copy in halo_copies + weight_copies:
        copy.wait_send()
    arrived.wait_send()
    for k in range(heads):

        @pl.when(half * heads + k != me_c)
        def _():
            back(k).wait_send()


def shards(latent, conv_weight, conv_gain, qkv_weight, qk_gain, out_weight):
    images, tile_rows, tile_cols, channels = latent.shape
    layers = conv_weight.shape[0]
    row_count, col_count = lax.axis_size("row"), lax.axis_size("col")
    devices = row_count * col_count
    sizes = (images, tile_rows, tile_cols, layers, row_count, col_count)
    pack, place, read, segments = plan(images, tile_rows, tile_cols, layers)
    own_count, border_count = pack.shape[1], pack.shape[0]
    tile_tokens = tile_rows * tile_cols // 4
    image_tokens = devices * tile_tokens
    strip = row_count * tile_tokens
    heads = col_count // 2
    half_rows = qkv_weight.shape[1]
    ext_count = place.shape[0]
    bf16, f32 = jnp.bfloat16, jnp.float32
    vmem, anywhere = pl.BlockSpec(memory_space=pltpu.VMEM), pl.BlockSpec(memory_space=pl.ANY)
    dma = pltpu.SemaphoreType.DMA
    features, mixed = pl.pallas_call(
        functools.partial(kernel, sizes, segments),
        out_shape=(
            jax.ShapeDtypeStruct((own_count, channels), bf16),
            jax.ShapeDtypeStruct((strip, channels), bf16),
        ),
        in_specs=[vmem, anywhere, vmem, anywhere, vmem, anywhere, vmem, vmem, vmem],
        out_specs=(vmem, vmem),
        scratch_shapes=[
            pltpu.VMEM(conv_weight.shape, bf16),
            pltpu.VMEM((3, ext_count, channels), bf16),
            pltpu.VMEM((border_count, channels), bf16),
            pltpu.VMEM((own_count + border_count, channels), bf16),
            pltpu.VMEM((2,) + qkv_weight.shape, bf16),
            pltpu.VMEM((2,) + out_weight.shape, bf16),
            pltpu.VMEM((2, 8, 2 * half_rows), f32),
            pltpu.VMEM((images, tile_tokens, channels), f32),
            pltpu.VMEM((devices, tile_tokens, channels), f32),
            pltpu.VMEM((image_tokens, channels), f32),
            pltpu.VMEM((heads, strip, channels), bf16),
            pltpu.VMEM((heads, strip, channels), bf16),
            dma((layers * 3,)),
            dma((2,)),
            dma((len(SIDES),)),
            dma((len(SIDES),)),
            dma((3,)),
            dma((3,)),
            dma,
            dma,
            dma((heads,)),
            dma((heads,)),
        ],
        compiler_params=pltpu.CompilerParams(
            collective_id=0, has_side_effects=True, vmem_limit_bytes=56 * 1024 * 1024
        ),
    )(
        latent.reshape(own_count, channels),
        conv_weight,
        conv_gain,
        qkv_weight,
        qk_gain,
        out_weight,
        jnp.asarray(pack, bf16),
        jnp.asarray(place, bf16),
        jnp.asarray(read, bf16),
    )
    return (
        features.reshape(latent.shape),
        mixed.reshape(1, row_count * tile_rows // 2, tile_cols // 2, channels),
    )


def solution(mesh):
    placed = (
        P(None, "row", "col", None),
        P(),
        P(),
        P(None, "col", None),
        P(None, "col"),
        P("col", None),
    )
    return jax.shard_map(
        shards,
        mesh=mesh,
        in_specs=placed,
        out_specs=(P(None, "row", "col", None), P("row", None, "col", None)),
        check_vma=False,
    )
```

```python
import functools

import jax
import jax.numpy as jnp
import numpy as np
from jax import lax
from jax.experimental import pallas as pl
from jax.experimental.pallas import tpu as pltpu
from jax.sharding import PartitionSpec as P

MESH = pl.DeviceIdType.MESH
SIDES = [(0, 1), (0, -1), (1, 0), (-1, 0), (1, 1), (1, -1), (-1, 1), (-1, -1)]


def edge_source(step, tile, width):
    return {-1: range(width), 1: range(tile - width, tile), 0: range(tile)}[step]


def edge_target(step, tile, width):
    return {
        -1: range(width + tile, tile + 2 * width),
        1: range(width),
        0: range(width, width + tile),
    }[step]


def plan(images, tile_rows, tile_cols, width):
    ext_rows, ext_cols = tile_rows + 2 * width, tile_cols + 2 * width
    own_count = images * tile_rows * tile_cols

    def own_at(n, i, j):
        return (n * tile_rows + i) * tile_cols + j

    def ext_at(n, i, j):
        return (i * images + n) * ext_cols + j

    pack, segments, placed = [], [], np.zeros(images * ext_rows * ext_cols, np.int64)
    for n in range(images):
        for i in range(tile_rows):
            for j in range(tile_cols):
                placed[ext_at(n, i + width, j + width)] = own_at(n, i, j)
    for dr, dc in SIDES:
        start = len(pack)
        pairs = zip(edge_source(dr, tile_rows, width), edge_target(dr, tile_rows, width))
        for i, ti in pairs:
            for n in range(images):
                cols = zip(edge_source(dc, tile_cols, width), edge_target(dc, tile_cols, width))
                for j, tj in cols:
                    placed[ext_at(n, ti, tj)] = own_count + len(pack)
                    pack.append(own_at(n, i, j))
        segments.append((start, len(pack) - start))
    pack_matrix = np.eye(own_count)[np.array(pack)]
    place_matrix = np.eye(own_count + len(pack))[placed]
    read = np.zeros((own_count + own_count // 4, images * tile_rows * ext_cols))
    for n in range(images):
        for i in range(tile_rows):
            for j in range(tile_cols):
                at = ext_at(n, i, j + width)
                read[own_at(n, i, j), at] = 1.0
                token = (n * (tile_rows // 2) + i // 2) * (tile_cols // 2) + j // 2
                read[own_count + token, at] = 0.25
    return pack_matrix, place_matrix, read, segments


def dot(a, b):
    return jnp.dot(a, b, preferred_element_type=jnp.float32)


def dot_t(a, b):
    return lax.dot_general(a, b, (((1,), (1,)), ((), ())), preferred_element_type=jnp.float32)


def kernel(
    sizes,
    segments,
    latent_ref, conv_hbm, gain_ref, qkv_hbm, qk_gain_ref, out_hbm, pack_ref, place_ref, read_ref,
    features_hbm, mixed_hbm,
    conv_w, shifted_act, border, around, qkv_w, out_w, head_gain, pooled_own, pooled_row,
    strips, terms, returned, own_rows, features, mixed,
    conv_sem, local_sem, out_sem, halo_send, halo_recv, weight_send, weight_recv,
    row_send, row_recv, col_send, col_recv, back_send, back_recv,
):
    images, tile_rows, tile_cols, layers, row_count, col_count = sizes
    ext_rows, ext_cols = tile_rows + 2 * layers, tile_cols + 2 * layers
    channels = latent_ref.shape[-1]
    own_count = images * tile_rows * tile_cols
    me_r, me_c = lax.axis_index("row"), lax.axis_index("col")
    half = lax.rem(me_c, 2)
    head = me_c // 2
    partner = (me_r, me_c + 1 - 2 * half)

    def in_row(step):
        return lax.rem(me_r + step, row_count), me_c

    def in_col(step):
        return me_r, lax.rem(me_c + step, col_count)

    barrier = pltpu.get_barrier_semaphore()

    peers = [in_row(step) for step in range(1, row_count)]
    peers += [in_col(step) for step in range(1, col_count)]
    for dr, dc in SIDES[4:]:
        peers.append((in_row(row_count + dr)[0], in_col(col_count + dc)[1]))
    for peer in peers:
        pl.semaphore_signal(barrier, inc=1, device_id=peer, device_id_type=MESH)
    own_qkv = pltpu.make_async_copy(qkv_hbm, qkv_w.at[half], local_sem.at[0])
    own_out = pltpu.make_async_copy(out_hbm, out_w.at[half], local_sem.at[1])
    own_qkv.start()
    own_out.start()
    conv_copies = []
    for layer in range(layers):
        for a in range(3):
            at = layer * 3 + a
            copy = pltpu.make_async_copy(conv_hbm.at[layer, a], conv_w.at[layer, a], conv_sem.at[at])
            copy.start()
            conv_copies.append(copy)

    for n in range(images):
        for i in range(tile_rows):
            at = (n * tile_rows + i) * tile_cols
            own_rows[at : at + tile_cols] = latent_ref[n, i].astype(jnp.float32)
    own = own_rows[...].astype(jnp.bfloat16)
    border[...] = dot(pack_ref[...], own).astype(jnp.bfloat16)
    around[:own_count] = own
    head_gain[half] = jnp.zeros(head_gain.shape[1:], jnp.float32)
    head_gain[half, :2, : qk_gain_ref.shape[1]] = qk_gain_ref[...].astype(jnp.float32)
    pl.semaphore_wait(barrier, len(peers))

    halo_copies = []
    for k, (dr, dc) in enumerate(SIDES):
        start, count = segments[k]
        to = (lax.rem(me_r + dr + row_count, row_count), lax.rem(me_c + dc + col_count, col_count))
        copy = pltpu.make_async_remote_copy(
            src_ref=border.at[pl.ds(start, count)],
            dst_ref=around.at[pl.ds(own_count + start, count)],
            send_sem=halo_send.at[k],
            recv_sem=halo_recv.at[k],
            device_id=to,
            device_id_type=MESH,
        )
        copy.start()
        halo_copies.append(copy)
    own_qkv.wait()
    own_out.wait()
    weight_copies = []
    for k, ref in enumerate((qkv_w, out_w, head_gain)):
        copy = pltpu.make_async_remote_copy(
            src_ref=ref.at[half],
            dst_ref=ref.at[half],
            send_sem=weight_send.at[k],
            recv_sem=weight_recv.at[k],
            device_id=partner,
            device_id_type=MESH,
        )
        copy.start()
        weight_copies.append(copy)
    for copy in halo_copies:
        copy.wait_recv()

    hidden = dot(place_ref[...], around[...])
    line = images * ext_cols
    for layer in range(layers):
        factor = lax.rsqrt(jnp.mean(hidden * hidden, axis=-1, keepdims=True) + 1e-06)
        act = jax.nn.silu(hidden * factor * gain_ref[layer : layer + 1, :])
        rows = act.shape[0]
        groups = act.reshape(rows // ext_cols, ext_cols, channels)
        for b in range(3):
            moved = groups if b == 1 else pltpu.roll(groups, (1 - b) % ext_cols, axis=1)
            shifted_act[b, :rows] = moved.reshape(rows, channels).astype(jnp.bfloat16)
        inner = rows - 2 * line
        total = jnp.zeros((inner, channels), jnp.float32)
        for a in range(3):
            conv_copies[layer * 3 + a].wait()
            for b in range(3):
                total = total + dot(shifted_act[b, a * line : a * line + inner], conv_w[layer, a, b])
        rounded = (hidden[line : line + inner] + total).astype(jnp.bfloat16)
        hidden = rounded.astype(jnp.float32)

    both = dot(read_ref[...], rounded)
    pooled = both[own_count:].astype(jnp.bfloat16).astype(jnp.float32)
    tile_tokens = pooled_own.shape[1]
    for n in range(images):
        pooled_own[n] = pooled[n * tile_tokens : (n + 1) * tile_tokens]

    for step in range(1, row_count):
        to = in_row(step)
        pltpu.make_async_remote_copy(
            src_ref=pooled_own.at[to[0]],
            dst_ref=pooled_row.at[me_r],
            send_sem=row_send,
            recv_sem=row_recv,
            device_id=to,
            device_id_type=MESH,
        ).start()
    pooled_row[me_r] = pooled_own[me_r]
    for n in range(images):
        for i in range(tile_rows):
            at = (n * tile_rows + i) * tile_cols
            features[n, i] = both[at : at + tile_cols].astype(jnp.bfloat16)
    features_out = pltpu.make_async_copy(features, features_hbm, out_sem.at[0])
    features_out.start()
    row_arrived = pltpu.make_async_remote_copy(
        src_ref=pooled_row.at[pl.ds(0, row_count - 1)],
        dst_ref=pooled_row.at[pl.ds(0, row_count - 1)],
        send_sem=row_send,
        recv_sem=row_recv,
        device_id=partner,
        device_id_type=MESH,
    )
    row_arrived.wait_recv()

    mine = jnp.concatenate([pooled_row[r] for r in range(row_count)], axis=0)
    strips[me_c] = mine.astype(jnp.bfloat16)
    for step in range(1, col_count):
        pltpu.make_async_remote_copy(
            src_ref=strips.at[me_c],
            dst_ref=strips.at[me_c],
            send_sem=col_send,
            recv_sem=col_recv,
            device_id=in_col(step),
            device_id_type=MESH,
        ).start()
    for copy in weight_copies:
        copy.wait_recv()
    col_arrived = pltpu.make_async_remote_copy(
        src_ref=strips.at[pl.ds(0, col_count - 1)],
        dst_ref=strips.at[pl.ds(0, col_count - 1)],
        send_sem=col_send,
        recv_sem=col_recv,
        device_id=partner,
        device_id_type=MESH,
    )
    col_arrived.wait_recv()

    head_dim = 2 * qkv_w.shape[2]

    def head_matrix(part):
        return qkv_w[:, part].reshape(head_dim, channels)

    gains = head_gain[0] + pltpu.roll(head_gain[1], head_dim // 2, axis=1)

    def head_norm(projected, gain_row):
        factor = lax.rsqrt(jnp.mean(projected * projected, axis=-1, keepdims=True) + 1e-06)
        return (projected * factor * gain_row).astype(jnp.bfloat16)

    strip = terms.shape[1]
    count = col_count * strip
    queries = count // 2
    image_tokens = strips[...].reshape(count, channels)
    key_norm = head_norm(dot_t(image_tokens, head_matrix(1)), gains[1:2])
    value_rows = dot_t(image_tokens, head_matrix(2)).astype(jnp.bfloat16)
    block = min(queries, 128)

    def attend(at):
        first = half * (col_count // 2) + at * (block // strip)
        rows = strips[pl.ds(first, block // strip)].reshape(block, channels)
        query_norm = head_norm(dot_t(rows, head_matrix(0)), gains[0:1])
        scores = dot_t(query_norm, key_norm) * head_dim ** (-0.5)
        shifted = jnp.exp(scores - jnp.max(scores, axis=1, keepdims=True))
        out = dot(shifted.astype(jnp.bfloat16), value_rows)
        return (out / jnp.sum(shifted, axis=1, keepdims=True)).astype(jnp.bfloat16)

    out_rows = out_w[...].reshape(head_dim, channels)

    def one_block(at):
        term = dot(attend(at), out_rows).astype(jnp.bfloat16)
        for k in range(block // strip):
            terms[at * (block // strip) + k] = term[k * strip : (k + 1) * strip]

    if queries == block:
        one_block(0)
    else:

        def step(at, _):
            one_block(at)
            return 0

        lax.fori_loop(0, queries // block, step, 0)

    heads = col_count // 2

    def back(k):
        return pltpu.make_async_remote_copy(
            src_ref=terms.at[k],
            dst_ref=returned.at[head],
            send_sem=back_send.at[k],
            recv_sem=back_recv.at[head],
            device_id=(me_r, half * heads + k),
            device_id_type=MESH,
        )

    for k in range(heads):

        @pl.when(half * heads + k != me_c)
        def _():
            back(k).start()

        @pl.when(half * heads + k == me_c)
        def _():
            returned[head] = terms[k]

    for h in range(heads):

        @pl.when(2 * h + me_c // heads != me_c)
        def _():
            pltpu.make_async_remote_copy(
                src_ref=terms.at[0],
                dst_ref=returned.at[h],
                send_sem=back_send.at[0],
                recv_sem=back_recv.at[h],
                device_id=partner,
                device_id_type=MESH,
            ).wait_recv()

    total = returned[0].astype(jnp.float32)
    for h in range(1, heads):
        total = total + returned[h].astype(jnp.float32)
    total = mine + total
    for t in range(mixed.shape[1]):
        width = mixed.shape[2]
        mixed[0, t] = total[t * width : (t + 1) * width].astype(jnp.bfloat16)
    mixed_out = pltpu.make_async_copy(mixed, mixed_hbm, out_sem.at[1])
    mixed_out.start()

    for copy in halo_copies + weight_copies:
        copy.wait_send()
    row_arrived.wait_send()
    col_arrived.wait_send()
    for k in range(heads):

        @pl.when(half * heads + k != me_c)
        def _():
            back(k).wait_send()

    features_out.wait()
    mixed_out.wait()


def shards(latent, conv_weight, conv_gain, qkv_weight, qk_gain, out_weight):
    images, tile_rows, tile_cols, channels = latent.shape
    layers = conv_weight.shape[0]
    row_count, col_count = lax.axis_size("row"), lax.axis_size("col")
    sizes = (images, tile_rows, tile_cols, layers, row_count, col_count)
    pack, place, read, segments = plan(images, tile_rows, tile_cols, layers)
    own_count, border_count = pack.shape[1], pack.shape[0]
    tile_tokens = tile_rows * tile_cols // 4
    strip = row_count * tile_tokens
    heads = col_count // 2
    half_rows = qkv_weight.shape[1]
    ext_count = place.shape[0]
    bf16, f32 = jnp.bfloat16, jnp.float32
    vmem, anywhere = pl.BlockSpec(memory_space=pltpu.VMEM), pl.BlockSpec(memory_space=pl.ANY)
    dma = pltpu.SemaphoreType.DMA
    mixed_shape = (1, row_count * tile_rows // 2, tile_cols // 2, channels)
    return pl.pallas_call(
        functools.partial(kernel, sizes, segments),
        out_shape=(
            jax.ShapeDtypeStruct(latent.shape, bf16),
            jax.ShapeDtypeStruct(mixed_shape, bf16),
        ),
        in_specs=[vmem, anywhere, vmem, anywhere, vmem, anywhere, vmem, vmem, vmem],
        out_specs=(anywhere, anywhere),
        scratch_shapes=[
            pltpu.VMEM(conv_weight.shape, bf16),
            pltpu.VMEM((3, ext_count, channels), bf16),
            pltpu.VMEM((border_count, channels), bf16),
            pltpu.VMEM((own_count + border_count, channels), bf16),
            pltpu.VMEM((2,) + qkv_weight.shape, bf16),
            pltpu.VMEM((2,) + out_weight.shape, bf16),
            pltpu.VMEM((2, 8, 2 * half_rows), f32),
            pltpu.VMEM((images, tile_tokens, channels), f32),
            pltpu.VMEM((row_count, tile_tokens, channels), f32),
            pltpu.VMEM((col_count, strip, channels), bf16),
            pltpu.VMEM((heads, strip, channels), bf16),
            pltpu.VMEM((heads, strip, channels), bf16),
            pltpu.VMEM((own_count, channels), f32),
            pltpu.VMEM(latent.shape, bf16),
            pltpu.VMEM(mixed_shape, bf16),
            dma((layers * 3,)),
            dma((2,)),
            dma((2,)),
            dma((len(SIDES),)),
            dma((len(SIDES),)),
            dma((3,)),
            dma((3,)),
            dma,
            dma,
            dma,
            dma,
            dma((heads,)),
            dma((heads,)),
        ],
        compiler_params=pltpu.CompilerParams(
            collective_id=0, has_side_effects=True, vmem_limit_bytes=56 * 1024 * 1024
        ),
    )(
        latent,
        conv_weight,
        conv_gain,
        qkv_weight,
        qk_gain,
        out_weight,
        jnp.asarray(pack, bf16),
        jnp.asarray(place, bf16),
        jnp.asarray(read, bf16),
    )


def solution(mesh):
    placed = (
        P(None, "row", "col", None),
        P(),
        P(),
        P(None, "col", None),
        P(None, "col"),
        P("col", None),
    )
    return jax.shard_map(
        shards,
        mesh=mesh,
        in_specs=placed,
        out_specs=(P(None, "row", "col", None), P("row", None, "col", None)),
        check_vma=False,
    )
```

```python
import functools

import jax
import jax.numpy as jnp
import numpy as np
from jax import lax
from jax.experimental import pallas as pl
from jax.experimental.pallas import tpu as pltpu
from jax.sharding import PartitionSpec as P

MESH = pl.DeviceIdType.MESH
SIDES = [(0, 1), (0, -1), (1, 0), (-1, 0), (1, 1), (1, -1), (-1, 1), (-1, -1)]


def edge_source(step, tile, width):
    return {-1: range(width), 1: range(tile - width, tile), 0: range(tile)}[step]


def edge_target(step, tile, width):
    return {
        -1: range(width + tile, tile + 2 * width),
        1: range(width),
        0: range(width, width + tile),
    }[step]


def plan(images, tile_rows, tile_cols, width):
    ext_rows, ext_cols = tile_rows + 2 * width, tile_cols + 2 * width
    own_count = images * tile_rows * tile_cols

    def own_at(n, i, j):
        return (n * tile_rows + i) * tile_cols + j

    def ext_at(n, i, j):
        return (i * images + n) * ext_cols + j

    pack, segments, placed = [], [], np.zeros(images * ext_rows * ext_cols, np.int64)
    for n in range(images):
        for i in range(tile_rows):
            for j in range(tile_cols):
                placed[ext_at(n, i + width, j + width)] = own_at(n, i, j)
    for dr, dc in SIDES:
        start = len(pack)
        pairs = zip(edge_source(dr, tile_rows, width), edge_target(dr, tile_rows, width))
        for i, ti in pairs:
            for n in range(images):
                cols = zip(edge_source(dc, tile_cols, width), edge_target(dc, tile_cols, width))
                for j, tj in cols:
                    placed[ext_at(n, ti, tj)] = own_count + len(pack)
                    pack.append(own_at(n, i, j))
        segments.append((start, len(pack) - start))
    pack_matrix = np.eye(own_count)[np.array(pack)]
    place_matrix = np.eye(own_count + len(pack))[placed]
    read = np.zeros((own_count + own_count // 4, images * tile_rows * ext_cols))
    for n in range(images):
        for i in range(tile_rows):
            for j in range(tile_cols):
                at = ext_at(n, i, j + width)
                read[own_at(n, i, j), at] = 1.0
                token = (n * (tile_rows // 2) + i // 2) * (tile_cols // 2) + j // 2
                read[own_count + token, at] = 0.25
    return pack_matrix, place_matrix, read, segments


def dot(a, b):
    return jnp.dot(a, b, preferred_element_type=jnp.float32)


def dot_t(a, b):
    return lax.dot_general(a, b, (((1,), (1,)), ((), ())), preferred_element_type=jnp.float32)


def kernel(
    sizes,
    segments,
    latent_ref, conv_hbm, gain_ref, qkv_hbm, qk_gain_ref, out_hbm, pack_ref, place_ref, read_ref,
    features_hbm, mixed_hbm,
    conv_w, shifted_act, border, around, qkv_w, out_w, head_gain, pooled_own, pooled_row,
    strips, terms, returned, own_rows, features, mixed,
    conv_sem, local_sem, out_sem, halo_send, halo_recv, weight_send, weight_recv,
    row_send, row_recv, col_send, col_recv, back_send, back_recv,
):
    images, tile_rows, tile_cols, layers, row_count, col_count = sizes
    ext_rows, ext_cols = tile_rows + 2 * layers, tile_cols + 2 * layers
    channels = latent_ref.shape[-1]
    own_count = images * tile_rows * tile_cols
    lanes = conv_w.shape[2] // 3
    me_r, me_c = lax.axis_index("row"), lax.axis_index("col")
    half = lax.rem(me_c, 2)
    head = me_c // 2
    partner = (me_r, me_c + 1 - 2 * half)

    def in_row(step):
        return lax.rem(me_r + step, row_count), me_c

    def in_col(step):
        return me_r, lax.rem(me_c + step, col_count)

    barrier = pltpu.get_barrier_semaphore()

    peers = [in_row(step) for step in range(1, row_count)]
    peers += [in_col(step) for step in range(1, col_count)]
    for dr, dc in SIDES[4:]:
        peers.append((in_row(row_count + dr)[0], in_col(col_count + dc)[1]))
    for peer in peers:
        pl.semaphore_signal(barrier, inc=1, device_id=peer, device_id_type=MESH)
    own_qkv = pltpu.make_async_copy(qkv_hbm, qkv_w.at[half], local_sem.at[0])
    own_out = pltpu.make_async_copy(out_hbm, out_w.at[half], local_sem.at[1])
    own_qkv.start()
    own_out.start()
    conv_copies = []
    for layer in range(layers):
        for a in range(3):
            for b in range(3):
                copy = pltpu.make_async_copy(
                    conv_hbm.at[layer, a, b],
                    conv_w.at[layer, a, pl.ds(b * lanes, channels)],
                    conv_sem.at[len(conv_copies)],
                )
                copy.start()
                conv_copies.append(copy)
                if lanes > channels:
                    conv_w[layer, a, b * lanes + channels : (b + 1) * lanes] = jnp.zeros(
                        (lanes - channels, channels), jnp.bfloat16
                    )
    if lanes > channels:
        shifted_act[...] = jnp.zeros_like(shifted_act)

    for n in range(images):
        for i in range(tile_rows):
            at = (n * tile_rows + i) * tile_cols
            own_rows[at : at + tile_cols] = latent_ref[n, i].astype(jnp.float32)
    own = own_rows[...].astype(jnp.bfloat16)
    border[...] = dot(pack_ref[...], own).astype(jnp.bfloat16)
    around[:own_count] = own
    head_gain[half] = jnp.zeros(head_gain.shape[1:], jnp.float32)
    head_gain[half, :2, : qk_gain_ref.shape[1]] = qk_gain_ref[...].astype(jnp.float32)
    pl.semaphore_wait(barrier, len(peers))

    halo_copies = []
    for k, (dr, dc) in enumerate(SIDES):
        start, count = segments[k]
        to = (lax.rem(me_r + dr + row_count, row_count), lax.rem(me_c + dc + col_count, col_count))
        copy = pltpu.make_async_remote_copy(
            src_ref=border.at[pl.ds(start, count)],
            dst_ref=around.at[pl.ds(own_count + start, count)],
            send_sem=halo_send.at[k],
            recv_sem=halo_recv.at[k],
            device_id=to,
            device_id_type=MESH,
        )
        copy.start()
        halo_copies.append(copy)
    own_qkv.wait()
    own_out.wait()
    weight_copies = []
    for k, ref in enumerate((qkv_w, out_w, head_gain)):
        copy = pltpu.make_async_remote_copy(
            src_ref=ref.at[half],
            dst_ref=ref.at[half],
            send_sem=weight_send.at[k],
            recv_sem=weight_recv.at[k],
            device_id=partner,
            device_id_type=MESH,
        )
        copy.start()
        weight_copies.append(copy)
    for copy in halo_copies:
        copy.wait_recv()

    hidden = dot(place_ref[...], around[...])
    line = images * ext_cols
    for layer in range(layers):
        factor = lax.rsqrt(jnp.mean(hidden * hidden, axis=-1, keepdims=True) + 1e-06)
        act = jax.nn.silu(hidden * factor * gain_ref[layer : layer + 1, :])
        rows = act.shape[0]
        groups = act.reshape(rows // ext_cols, ext_cols, channels)
        for b in range(3):
            moved = groups if b == 1 else pltpu.roll(groups, (1 - b) % ext_cols, axis=1)
            shifted_act[:rows, b * lanes : b * lanes + channels] = moved.reshape(
                rows, channels
            ).astype(jnp.bfloat16)
        inner = rows - 2 * line
        total = jnp.zeros((inner, channels), jnp.float32)
        for a in range(3):
            for b in range(3):
                conv_copies[(layer * 3 + a) * 3 + b].wait()
            total = total + dot(shifted_act[a * line : a * line + inner], conv_w[layer, a])
        rounded = (hidden[line : line + inner] + total).astype(jnp.bfloat16)
        hidden = rounded.astype(jnp.float32)

    both = dot(read_ref[...], rounded)
    pooled = both[own_count:].astype(jnp.bfloat16).astype(jnp.float32)
    tile_tokens = pooled_own.shape[1]
    for n in range(images):
        pooled_own[n] = pooled[n * tile_tokens : (n + 1) * tile_tokens]

    for step in range(1, row_count):
        to = in_row(step)
        pltpu.make_async_remote_copy(
            src_ref=pooled_own.at[to[0]],
            dst_ref=pooled_row.at[me_r],
            send_sem=row_send,
            recv_sem=row_recv,
            device_id=to,
            device_id_type=MESH,
        ).start()
    pooled_row[me_r] = pooled_own[me_r]
    for n in range(images):
        for i in range(tile_rows):
            at = (n * tile_rows + i) * tile_cols
            features[n, i] = both[at : at + tile_cols].astype(jnp.bfloat16)
    features_out = pltpu.make_async_copy(features, features_hbm, out_sem.at[0])
    features_out.start()
    row_arrived = pltpu.make_async_remote_copy(
        src_ref=pooled_row.at[pl.ds(0, row_count - 1)],
        dst_ref=pooled_row.at[pl.ds(0, row_count - 1)],
        send_sem=row_send,
        recv_sem=row_recv,
        device_id=partner,
        device_id_type=MESH,
    )
    row_arrived.wait_recv()

    mine = jnp.concatenate([pooled_row[r] for r in range(row_count)], axis=0)
    strips[me_c] = mine.astype(jnp.bfloat16)
    for step in range(1, col_count):
        pltpu.make_async_remote_copy(
            src_ref=strips.at[me_c],
            dst_ref=strips.at[me_c],
            send_sem=col_send,
            recv_sem=col_recv,
            device_id=in_col(step),
            device_id_type=MESH,
        ).start()
    for copy in weight_copies:
        copy.wait_recv()
    col_arrived = pltpu.make_async_remote_copy(
        src_ref=strips.at[pl.ds(0, col_count - 1)],
        dst_ref=strips.at[pl.ds(0, col_count - 1)],
        send_sem=col_send,
        recv_sem=col_recv,
        device_id=partner,
        device_id_type=MESH,
    )
    col_arrived.wait_recv()

    head_dim = 2 * qkv_w.shape[2]

    def head_matrix(part):
        return qkv_w[:, part].reshape(head_dim, channels)

    gains = head_gain[0] + pltpu.roll(head_gain[1], head_dim // 2, axis=1)

    def head_norm(projected, gain_row):
        factor = lax.rsqrt(jnp.mean(projected * projected, axis=-1, keepdims=True) + 1e-06)
        return (projected * factor * gain_row).astype(jnp.bfloat16)

    strip = terms.shape[1]
    count = col_count * strip
    queries = count // 2
    image_tokens = strips[...].reshape(count, channels)
    key_norm = head_norm(dot_t(image_tokens, head_matrix(1)), gains[1:2])
    value_rows = dot_t(image_tokens, head_matrix(2)).astype(jnp.bfloat16)
    block = min(queries, 128)

    def attend(at):
        first = half * (col_count // 2) + at * (block // strip)
        rows = strips[pl.ds(first, block // strip)].reshape(block, channels)
        query_norm = head_norm(dot_t(rows, head_matrix(0)), gains[0:1])
        scores = dot_t(query_norm, key_norm) * head_dim ** (-0.5)
        shifted = jnp.exp(scores - jnp.max(scores, axis=1, keepdims=True))
        out = dot(shifted.astype(jnp.bfloat16), value_rows)
        return (out / jnp.sum(shifted, axis=1, keepdims=True)).astype(jnp.bfloat16)

    out_rows = out_w[...].reshape(head_dim, channels)

    def one_block(at):
        term = dot(attend(at), out_rows).astype(jnp.bfloat16)
        for k in range(block // strip):
            terms[at * (block // strip) + k] = term[k * strip : (k + 1) * strip]

    if queries == block:
        one_block(0)
    else:

        def step(at, _):
            one_block(at)
            return 0

        lax.fori_loop(0, queries // block, step, 0)

    heads = col_count // 2

    def back(k):
        return pltpu.make_async_remote_copy(
            src_ref=terms.at[k],
            dst_ref=returned.at[head],
            send_sem=back_send.at[k],
            recv_sem=back_recv.at[head],
            device_id=(me_r, half * heads + k),
            device_id_type=MESH,
        )

    for k in range(heads):

        @pl.when(half * heads + k != me_c)
        def _():
            back(k).start()

        @pl.when(half * heads + k == me_c)
        def _():
            returned[head] = terms[k]

    for h in range(heads):

        @pl.when(2 * h + me_c // heads != me_c)
        def _():
            pltpu.make_async_remote_copy(
                src_ref=terms.at[0],
                dst_ref=returned.at[h],
                send_sem=back_send.at[0],
                recv_sem=back_recv.at[h],
                device_id=partner,
                device_id_type=MESH,
            ).wait_recv()

    total = returned[0].astype(jnp.float32)
    for h in range(1, heads):
        total = total + returned[h].astype(jnp.float32)
    total = mine + total
    for t in range(mixed.shape[1]):
        width = mixed.shape[2]
        mixed[0, t] = total[t * width : (t + 1) * width].astype(jnp.bfloat16)
    mixed_out = pltpu.make_async_copy(mixed, mixed_hbm, out_sem.at[1])
    mixed_out.start()

    for copy in halo_copies + weight_copies:
        copy.wait_send()
    row_arrived.wait_send()
    col_arrived.wait_send()
    for k in range(heads):

        @pl.when(half * heads + k != me_c)
        def _():
            back(k).wait_send()

    features_out.wait()
    mixed_out.wait()


def shards(latent, conv_weight, conv_gain, qkv_weight, qk_gain, out_weight):
    images, tile_rows, tile_cols, channels = latent.shape
    layers = conv_weight.shape[0]
    row_count, col_count = lax.axis_size("row"), lax.axis_size("col")
    sizes = (images, tile_rows, tile_cols, layers, row_count, col_count)
    pack, place, read, segments = plan(images, tile_rows, tile_cols, layers)
    own_count, border_count = pack.shape[1], pack.shape[0]
    tile_tokens = tile_rows * tile_cols // 4
    strip = row_count * tile_tokens
    heads = col_count // 2
    half_rows = qkv_weight.shape[1]
    ext_count = place.shape[0]
    lanes = -(-channels // 128) * 128
    bf16, f32 = jnp.bfloat16, jnp.float32
    vmem, anywhere = pl.BlockSpec(memory_space=pltpu.VMEM), pl.BlockSpec(memory_space=pl.ANY)
    dma = pltpu.SemaphoreType.DMA
    mixed_shape = (1, row_count * tile_rows // 2, tile_cols // 2, channels)
    return pl.pallas_call(
        functools.partial(kernel, sizes, segments),
        out_shape=(
            jax.ShapeDtypeStruct(latent.shape, bf16),
            jax.ShapeDtypeStruct(mixed_shape, bf16),
        ),
        in_specs=[vmem, anywhere, vmem, anywhere, vmem, anywhere, vmem, vmem, vmem],
        out_specs=(anywhere, anywhere),
        scratch_shapes=[
            pltpu.VMEM((layers, 3, 3 * lanes, channels), bf16),
            pltpu.VMEM((ext_count, 3 * lanes), bf16),
            pltpu.VMEM((border_count, channels), bf16),
            pltpu.VMEM((own_count + border_count, channels), bf16),
            pltpu.VMEM((2,) + qkv_weight.shape, bf16),
            pltpu.VMEM((2,) + out_weight.shape, bf16),
            pltpu.VMEM((2, 8, 2 * half_rows), f32),
            pltpu.VMEM((images, tile_tokens, channels), f32),
            pltpu.VMEM((row_count, tile_tokens, channels), f32),
            pltpu.VMEM((col_count, strip, channels), bf16),
            pltpu.VMEM((heads, strip, channels), bf16),
            pltpu.VMEM((heads, strip, channels), bf16),
            pltpu.VMEM((own_count, channels), f32),
            pltpu.VMEM(latent.shape, bf16),
            pltpu.VMEM(mixed_shape, bf16),
            dma((layers * 9,)),
            dma((2,)),
            dma((2,)),
            dma((len(SIDES),)),
            dma((len(SIDES),)),
            dma((3,)),
            dma((3,)),
            dma,
            dma,
            dma,
            dma,
            dma((heads,)),
            dma((heads,)),
        ],
        compiler_params=pltpu.CompilerParams(
            collective_id=0, has_side_effects=True, vmem_limit_bytes=56 * 1024 * 1024
        ),
    )(
        latent,
        conv_weight,
        conv_gain,
        qkv_weight,
        qk_gain,
        out_weight,
        jnp.asarray(pack, bf16),
        jnp.asarray(place, bf16),
        jnp.asarray(read, bf16),
    )


def solution(mesh):
    placed = (
        P(None, "row", "col", None),
        P(),
        P(),
        P(None, "col", None),
        P(None, "col"),
        P("col", None),
    )
    return jax.shard_map(
        shards,
        mesh=mesh,
        in_specs=placed,
        out_specs=(P(None, "row", "col", None), P("row", None, "col", None)),
        check_vma=False,
    )
```

```python
import functools

import jax
import jax.numpy as jnp
import numpy as np
from jax import lax
from jax.experimental import pallas as pl
from jax.experimental.pallas import tpu as pltpu
from jax.sharding import PartitionSpec as P

MESH = pl.DeviceIdType.MESH
SIDES = [(0, 1), (0, -1), (1, 0), (-1, 0), (1, 1), (1, -1), (-1, 1), (-1, -1)]


def edge_source(step, tile, width):
    return {-1: range(width), 1: range(tile - width, tile), 0: range(tile)}[step]


def edge_target(step, tile, width):
    return {
        -1: range(width + tile, tile + 2 * width),
        1: range(width),
        0: range(width, width + tile),
    }[step]


def plan(images, tile_rows, tile_cols, width):
    ext_rows, ext_cols = tile_rows + 2 * width, tile_cols + 2 * width
    own_count = images * tile_rows * tile_cols

    def own_at(n, i, j):
        return (n * tile_rows + i) * tile_cols + j

    def ext_at(n, i, j):
        return (i * images + n) * ext_cols + j

    pack, segments, placed = [], [], np.zeros(images * ext_rows * ext_cols, np.int64)
    for n in range(images):
        for i in range(tile_rows):
            for j in range(tile_cols):
                placed[ext_at(n, i + width, j + width)] = own_at(n, i, j)
    for dr, dc in SIDES:
        start = len(pack)
        pairs = zip(edge_source(dr, tile_rows, width), edge_target(dr, tile_rows, width))
        for i, ti in pairs:
            for n in range(images):
                cols = zip(edge_source(dc, tile_cols, width), edge_target(dc, tile_cols, width))
                for j, tj in cols:
                    placed[ext_at(n, ti, tj)] = own_count + len(pack)
                    pack.append(own_at(n, i, j))
        segments.append((start, len(pack) - start))
    pack_matrix = np.eye(own_count)[np.array(pack)]
    place_matrix = np.eye(own_count + len(pack))[placed]
    read = np.zeros((own_count + own_count // 4, images * tile_rows * ext_cols))
    for n in range(images):
        for i in range(tile_rows):
            for j in range(tile_cols):
                at = ext_at(n, i, j + width)
                read[own_at(n, i, j), at] = 1.0
                token = (n * (tile_rows // 2) + i // 2) * (tile_cols // 2) + j // 2
                read[own_count + token, at] = 0.25
    return pack_matrix, place_matrix, read, segments


def dot(a, b):
    return jnp.dot(a, b, preferred_element_type=jnp.float32)


def dot_t(a, b):
    return lax.dot_general(a, b, (((1,), (1,)), ((), ())), preferred_element_type=jnp.float32)


def kernel(
    sizes,
    segments,
    latent_hbm, conv_hbm, gain_hbm, qkv_hbm, qk_gain_hbm, out_hbm, pack_hbm, place_hbm, read_hbm,
    features_hbm, mixed_hbm,
    conv_w, shifted_act, border, around, qkv_w, out_w, head_gain, pooled_own, pooled_row,
    strips, terms, returned, own_rows, features, mixed,
    latent_ref, gain_ref, qk_gain_ref, pack_ref, place_ref, read_ref, small_sem,
    conv_sem, local_sem, out_sem, halo_send, halo_recv, weight_send, weight_recv,
    row_send, row_recv, col_send, col_recv, back_send, back_recv,
):
    images, tile_rows, tile_cols, layers, row_count, col_count = sizes
    ext_rows, ext_cols = tile_rows + 2 * layers, tile_cols + 2 * layers
    channels = latent_ref.shape[-1]
    own_count = images * tile_rows * tile_cols
    lanes = conv_w.shape[2] // 3
    me_r, me_c = lax.axis_index("row"), lax.axis_index("col")
    half = lax.rem(me_c, 2)
    head = me_c // 2
    partner = (me_r, me_c + 1 - 2 * half)

    def in_row(step):
        return lax.rem(me_r + step, row_count), me_c

    def in_col(step):
        return me_r, lax.rem(me_c + step, col_count)

    barrier = pltpu.get_barrier_semaphore()

    peers = [in_row(step) for step in range(1, row_count)]
    peers += [in_col(step) for step in range(1, col_count)]
    for dr, dc in SIDES[4:]:
        peers.append((in_row(row_count + dr)[0], in_col(col_count + dc)[1]))
    for peer in peers:
        pl.semaphore_signal(barrier, inc=1, device_id=peer, device_id_type=MESH)
    small_copies = []
    for source, target in (
        (latent_hbm, latent_ref),
        (pack_hbm, pack_ref),
        (qk_gain_hbm, qk_gain_ref),
        (place_hbm, place_ref),
        (gain_hbm, gain_ref),
        (read_hbm, read_ref),
    ):
        copy = pltpu.make_async_copy(source, target, small_sem.at[len(small_copies)])
        copy.start()
        small_copies.append(copy)
    own_qkv = pltpu.make_async_copy(qkv_hbm, qkv_w.at[half], local_sem.at[0])
    own_out = pltpu.make_async_copy(out_hbm, out_w.at[half], local_sem.at[1])
    own_qkv.start()
    own_out.start()
    conv_copies = []
    for layer in range(layers):
        for a in range(3):
            for b in range(3):
                copy = pltpu.make_async_copy(
                    conv_hbm.at[layer, a, b],
                    conv_w.at[layer, a, pl.ds(b * lanes, channels)],
                    conv_sem.at[len(conv_copies)],
                )
                copy.start()
                conv_copies.append(copy)
                if lanes > channels:
                    conv_w[layer, a, b * lanes + channels : (b + 1) * lanes] = jnp.zeros(
                        (lanes - channels, channels), jnp.bfloat16
                    )
    if lanes > channels:
        shifted_act[...] = jnp.zeros_like(shifted_act)
    for copy in small_copies:
        copy.wait()

    for n in range(images):
        for i in range(tile_rows):
            at = (n * tile_rows + i) * tile_cols
            own_rows[at : at + tile_cols] = latent_ref[n, i].astype(jnp.float32)
    own = own_rows[...].astype(jnp.bfloat16)
    border[...] = dot(pack_ref[...], own).astype(jnp.bfloat16)
    around[:own_count] = own
    head_gain[half] = jnp.zeros(head_gain.shape[1:], jnp.float32)
    head_gain[half, :2, : qk_gain_ref.shape[1]] = qk_gain_ref[...].astype(jnp.float32)
    pl.semaphore_wait(barrier, len(peers))

    halo_copies = []
    for k, (dr, dc) in enumerate(SIDES):
        start, count = segments[k]
        to = (lax.rem(me_r + dr + row_count, row_count), lax.rem(me_c + dc + col_count, col_count))
        copy = pltpu.make_async_remote_copy(
            src_ref=border.at[pl.ds(start, count)],
            dst_ref=around.at[pl.ds(own_count + start, count)],
            send_sem=halo_send.at[k],
            recv_sem=halo_recv.at[k],
            device_id=to,
            device_id_type=MESH,
        )
        copy.start()
        halo_copies.append(copy)
    own_qkv.wait()
    own_out.wait()
    weight_copies = []
    for k, ref in enumerate((qkv_w, out_w, head_gain)):
        copy = pltpu.make_async_remote_copy(
            src_ref=ref.at[half],
            dst_ref=ref.at[half],
            send_sem=weight_send.at[k],
            recv_sem=weight_recv.at[k],
            device_id=partner,
            device_id_type=MESH,
        )
        copy.start()
        weight_copies.append(copy)
    for copy in halo_copies:
        copy.wait_recv()

    hidden = dot(place_ref[...], around[...])
    line = images * ext_cols
    for layer in range(layers):
        factor = lax.rsqrt(jnp.mean(hidden * hidden, axis=-1, keepdims=True) + 1e-06)
        act = jax.nn.silu(hidden * factor * gain_ref[layer : layer + 1, :])
        rows = act.shape[0]
        groups = act.reshape(rows // ext_cols, ext_cols, channels)
        for b in range(3):
            moved = groups if b == 1 else pltpu.roll(groups, (1 - b) % ext_cols, axis=1)
            shifted_act[:rows, b * lanes : b * lanes + channels] = moved.reshape(
                rows, channels
            ).astype(jnp.bfloat16)
        inner = rows - 2 * line
        total = jnp.zeros((inner, channels), jnp.float32)
        for a in range(3):
            for b in range(3):
                conv_copies[(layer * 3 + a) * 3 + b].wait()
            total = total + dot(shifted_act[a * line : a * line + inner], conv_w[layer, a])
        rounded = (hidden[line : line + inner] + total).astype(jnp.bfloat16)
        hidden = rounded.astype(jnp.float32)

    both = dot(read_ref[...], rounded)
    pooled = both[own_count:].astype(jnp.bfloat16).astype(jnp.float32)
    tile_tokens = pooled_own.shape[1]
    for n in range(images):
        pooled_own[n] = pooled[n * tile_tokens : (n + 1) * tile_tokens]

    for step in range(1, row_count):
        to = in_row(step)
        pltpu.make_async_remote_copy(
            src_ref=pooled_own.at[to[0]],
            dst_ref=pooled_row.at[me_r],
            send_sem=row_send,
            recv_sem=row_recv,
            device_id=to,
            device_id_type=MESH,
        ).start()
    pooled_row[me_r] = pooled_own[me_r]
    for n in range(images):
        for i in range(tile_rows):
            at = (n * tile_rows + i) * tile_cols
            features[n, i] = both[at : at + tile_cols].astype(jnp.bfloat16)
    features_out = pltpu.make_async_copy(features, features_hbm, out_sem.at[0])
    features_out.start()
    row_arrived = pltpu.make_async_remote_copy(
        src_ref=pooled_row.at[pl.ds(0, row_count - 1)],
        dst_ref=pooled_row.at[pl.ds(0, row_count - 1)],
        send_sem=row_send,
        recv_sem=row_recv,
        device_id=partner,
        device_id_type=MESH,
    )
    row_arrived.wait_recv()

    mine = jnp.concatenate([pooled_row[r] for r in range(row_count)], axis=0)
    strips[me_c] = mine.astype(jnp.bfloat16)
    for step in range(1, col_count):
        pltpu.make_async_remote_copy(
            src_ref=strips.at[me_c],
            dst_ref=strips.at[me_c],
            send_sem=col_send,
            recv_sem=col_recv,
            device_id=in_col(step),
            device_id_type=MESH,
        ).start()
    for copy in weight_copies:
        copy.wait_recv()
    col_arrived = pltpu.make_async_remote_copy(
        src_ref=strips.at[pl.ds(0, col_count - 1)],
        dst_ref=strips.at[pl.ds(0, col_count - 1)],
        send_sem=col_send,
        recv_sem=col_recv,
        device_id=partner,
        device_id_type=MESH,
    )
    col_arrived.wait_recv()

    head_dim = 2 * qkv_w.shape[2]

    def head_matrix(part):
        return qkv_w[:, part].reshape(head_dim, channels)

    gains = head_gain[0] + pltpu.roll(head_gain[1], head_dim // 2, axis=1)

    def head_norm(projected, gain_row):
        factor = lax.rsqrt(jnp.mean(projected * projected, axis=-1, keepdims=True) + 1e-06)
        return (projected * factor * gain_row).astype(jnp.bfloat16)

    strip = terms.shape[1]
    count = col_count * strip
    queries = count // 2
    image_tokens = strips[...].reshape(count, channels)
    key_norm = head_norm(dot_t(image_tokens, head_matrix(1)), gains[1:2])
    value_rows = dot_t(image_tokens, head_matrix(2)).astype(jnp.bfloat16)
    block = min(queries, 128)

    def attend(at):
        first = half * (col_count // 2) + at * (block // strip)
        rows = strips[pl.ds(first, block // strip)].reshape(block, channels)
        query_norm = head_norm(dot_t(rows, head_matrix(0)), gains[0:1])
        scores = dot_t(query_norm, key_norm) * head_dim ** (-0.5)
        shifted = jnp.exp(scores - jnp.max(scores, axis=1, keepdims=True))
        out = dot(shifted.astype(jnp.bfloat16), value_rows)
        return (out / jnp.sum(shifted, axis=1, keepdims=True)).astype(jnp.bfloat16)

    out_rows = out_w[...].reshape(head_dim, channels)

    def one_block(at):
        term = dot(attend(at), out_rows).astype(jnp.bfloat16)
        for k in range(block // strip):
            terms[at * (block // strip) + k] = term[k * strip : (k + 1) * strip]

    if queries == block:
        one_block(0)
    else:

        def step(at, _):
            one_block(at)
            return 0

        lax.fori_loop(0, queries // block, step, 0)

    heads = col_count // 2

    def back(k):
        return pltpu.make_async_remote_copy(
            src_ref=terms.at[k],
            dst_ref=returned.at[head],
            send_sem=back_send.at[k],
            recv_sem=back_recv.at[head],
            device_id=(me_r, half * heads + k),
            device_id_type=MESH,
        )

    for k in range(heads):

        @pl.when(half * heads + k != me_c)
        def _():
            back(k).start()

        @pl.when(half * heads + k == me_c)
        def _():
            returned[head] = terms[k]

    for h in range(heads):

        @pl.when(2 * h + me_c // heads != me_c)
        def _():
            pltpu.make_async_remote_copy(
                src_ref=terms.at[0],
                dst_ref=returned.at[h],
                send_sem=back_send.at[0],
                recv_sem=back_recv.at[h],
                device_id=partner,
                device_id_type=MESH,
            ).wait_recv()

    total = returned[0].astype(jnp.float32)
    for h in range(1, heads):
        total = total + returned[h].astype(jnp.float32)
    total = mine + total
    for t in range(mixed.shape[1]):
        width = mixed.shape[2]
        mixed[0, t] = total[t * width : (t + 1) * width].astype(jnp.bfloat16)
    mixed_out = pltpu.make_async_copy(mixed, mixed_hbm, out_sem.at[1])
    mixed_out.start()

    for copy in halo_copies + weight_copies:
        copy.wait_send()
    row_arrived.wait_send()
    col_arrived.wait_send()
    for k in range(heads):

        @pl.when(half * heads + k != me_c)
        def _():
            back(k).wait_send()

    features_out.wait()
    mixed_out.wait()


def shards(latent, conv_weight, conv_gain, qkv_weight, qk_gain, out_weight):
    images, tile_rows, tile_cols, channels = latent.shape
    layers = conv_weight.shape[0]
    row_count, col_count = lax.axis_size("row"), lax.axis_size("col")
    sizes = (images, tile_rows, tile_cols, layers, row_count, col_count)
    pack, place, read, segments = plan(images, tile_rows, tile_cols, layers)
    own_count, border_count = pack.shape[1], pack.shape[0]
    tile_tokens = tile_rows * tile_cols // 4
    strip = row_count * tile_tokens
    heads = col_count // 2
    half_rows = qkv_weight.shape[1]
    ext_count = place.shape[0]
    lanes = -(-channels // 128) * 128
    bf16, f32 = jnp.bfloat16, jnp.float32
    anywhere = pl.BlockSpec(memory_space=pl.ANY)
    dma = pltpu.SemaphoreType.DMA
    mixed_shape = (1, row_count * tile_rows // 2, tile_cols // 2, channels)
    return pl.pallas_call(
        functools.partial(kernel, sizes, segments),
        out_shape=(
            jax.ShapeDtypeStruct(latent.shape, bf16),
            jax.ShapeDtypeStruct(mixed_shape, bf16),
        ),
        in_specs=[anywhere] * 9,
        out_specs=(anywhere, anywhere),
        scratch_shapes=[
            pltpu.VMEM((layers, 3, 3 * lanes, channels), bf16),
            pltpu.VMEM((ext_count, 3 * lanes), bf16),
            pltpu.VMEM((border_count, channels), bf16),
            pltpu.VMEM((own_count + border_count, channels), bf16),
            pltpu.VMEM((2,) + qkv_weight.shape, bf16),
            pltpu.VMEM((2,) + out_weight.shape, bf16),
            pltpu.VMEM((2, 8, 2 * half_rows), f32),
            pltpu.VMEM((images, tile_tokens, channels), f32),
            pltpu.VMEM((row_count, tile_tokens, channels), f32),
            pltpu.VMEM((col_count, strip, channels), bf16),
            pltpu.VMEM((heads, strip, channels), bf16),
            pltpu.VMEM((heads, strip, channels), bf16),
            pltpu.VMEM((own_count, channels), f32),
            pltpu.VMEM(latent.shape, bf16),
            pltpu.VMEM(mixed_shape, bf16),
            pltpu.VMEM(latent.shape, bf16),
            pltpu.VMEM(conv_gain.shape, f32),
            pltpu.VMEM(qk_gain.shape, bf16),
            pltpu.VMEM(pack.shape, bf16),
            pltpu.VMEM(place.shape, bf16),
            pltpu.VMEM(read.shape, bf16),
            dma((6,)),
            dma((layers * 9,)),
            dma((2,)),
            dma((2,)),
            dma((len(SIDES),)),
            dma((len(SIDES),)),
            dma((3,)),
            dma((3,)),
            dma,
            dma,
            dma,
            dma,
            dma((heads,)),
            dma((heads,)),
        ],
        compiler_params=pltpu.CompilerParams(
            collective_id=0, has_side_effects=True, vmem_limit_bytes=56 * 1024 * 1024
        ),
    )(
        latent,
        conv_weight,
        conv_gain,
        qkv_weight,
        qk_gain,
        out_weight,
        jnp.asarray(pack, bf16),
        jnp.asarray(place, bf16),
        jnp.asarray(read, bf16),
    )


def solution(mesh):
    placed = (
        P(None, "row", "col", None),
        P(),
        P(),
        P(None, "col", None),
        P(None, "col"),
        P("col", None),
    )
    return jax.shard_map(
        shards,
        mesh=mesh,
        in_specs=placed,
        out_specs=(P(None, "row", "col", None), P("row", None, "col", None)),
        check_vma=False,
    )
```
